768 devices in a mesh: dp: 32 (over x, y_hi, core), tensor: 24 (over y_lo, z).
Axes of the slice: x: 4, y: 8 (y_hi: 4, y_lo: 2; y = y_hi * 2 + y_lo), z: 12, core: 2. Of those that a mesh axis runs over, the one named last changes fastest.
Arguments:
- gate_pre: bfloat16 [9216, 15360], P('dp', 'tensor'), may hold values from -6 to 6
- up_pre: bfloat16 [9216, 15360], P('dp', 'tensor'), may hold values from -6 to 6
- down_weight: bfloat16 [15360, 4096], P('tensor'), may hold values from -0.046875 to 0.046875
- cotangent: bfloat16 [9216, 4096], P(('dp', 'tensor')), may hold values from -6 to 6
Outputs:
- output: bfloat16 [9216, 4096], P(('dp', 'tensor'))
- gate_grad: bfloat16 [9216, 15360], P('dp', 'tensor')
- up_grad: bfloat16 [9216, 15360], P('dp', 'tensor')
- weight_grad: bfloat16 [15360, 4096], P('tensor', 'dp')
The draws below stay inside these ranges and needn't reach their ends.
All inputs are finite; a program needn't handle non-finite values.
Results may differ from the reference program's by a relative error of at most 0.02.
Values may be sent and summed in bfloat16 or wider, within the bound.
No kernel may reach another device: no remote copies, remote signals or barrier semaphores. Data moves between devices by JAX's collectives and lax.ppermute only.
A program may use at most 64 MiB of HBM per device.

```python
import jax
import jax.numpy as jnp
from jax import lax

D = 4096
FF = 15360
TOK_DEV = 288
TOKENS = 9216
N_DP = 32
N_TENSOR = 24


def spiked(result, stream_key, source, target, parts, factor):
    def block_of(position):
        return (jnp.arange(result.shape[position]) // (result.shape[position] // parts)).reshape((-1,) + (1,) * (result.ndim - 1 - position))

    near = jax.random.permutation(stream_key, parts)[block_of(target)]
    far = (block_of(target) + parts // 2) % parts
    return jnp.where((block_of(source) == near) | (block_of(source) == far), factor * result, result)


def level_of(stream_key, extent, pieces, smallest, top_value):
    factor_of = 1.0
    for axis_at, parts in pieces:
        steps = jax.random.uniform(jax.random.fold_in(jax.random.fold_in(stream_key, 6), axis_at), (parts,), jnp.float32, smallest / len(pieces), top_value / len(pieces))
        factor_of = factor_of * jnp.repeat(jnp.exp(steps), extent[axis_at] // parts).reshape((-1,) + (1,) * (len(extent) - 1 - axis_at))
    return factor_of


def scatter_about(own_key, shape, scale, bound, pieces=(), dtype=jnp.bfloat16):
    result = jax.random.normal(own_key, shape, jnp.float32) * scale
    if len(pieces) > 0:
        result = level_of(own_key, shape, pieces, -0.22, 0.18) * result
    return jnp.clip(result, min=-bound, max=bound).astype(dtype)


def gaussian_with(own_key, extent, width, most, pieces, heavy, kind=jnp.bfloat16):
    result = width * jax.random.normal(own_key, extent, jnp.float32)
    if pieces:
        result = result * level_of(own_key, extent, pieces, -0.22, 0.18)
    return jnp.clip(spiked(result, jax.random.fold_in(own_key, 3), *heavy), -most, most).astype(kind)


def setup_inputs(seed: int = 0) -> dict:
    arg_keys = jax.random.split(jax.random.key(seed), 5)
    return {
        "gate_pre": scatter_about(arg_keys[0], (TOKENS, FF), 1.0, 6.0, ((0, 32), (1, 24))),
        "up_pre": gaussian_with(arg_keys[1], (TOKENS, FF), 1.0, 6.0, ((0, 32), (1, 24)), (1, 0, 32, 2.75)),
        "down_weight": scatter_about(arg_keys[2], (FF, D), FF ** -0.5, 0.046875, ((0, 24),)),
        "cotangent": scatter_about(arg_keys[3], (TOKENS, D), 1.0, 6.0, ((0, 768),)),
    }


def reference(gate_pre, up_pre, down_weight, cotangent):
    gate_groups = gate_pre.reshape(N_DP, TOK_DEV, FF)
    up_groups = up_pre.reshape(N_DP, TOK_DEV, FF)
    cot_groups = cotangent.reshape(N_DP, TOK_DEV, D)
    shard_width = FF // N_TENSOR
    weight_blocks = down_weight.reshape(N_TENSOR, shard_width, D)

    def one_group(grad_total, group_inputs):
        gate_rows, up_rows, cot_rows = group_inputs
        gate_wide = gate_rows.astype(jnp.float32)
        up_wide = up_rows.astype(jnp.float32)
        sigmoid_gate = jax.nn.sigmoid(gate_wide)
        activation = gate_wide * sigmoid_gate
        hidden = (activation * up_wide).astype(jnp.bfloat16)
        hidden_blocks = jnp.transpose(hidden.reshape(TOK_DEV, N_TENSOR, shard_width), (1, 0, 2))

        def add_block(out_total, block_inputs):
            hidden_block, weight_block = block_inputs
            partial_sum = jnp.dot(hidden_block, weight_block, preferred_element_type=jnp.float32)
            rounded_part = lax.optimization_barrier(partial_sum.astype(jnp.bfloat16))
            return out_total + rounded_part.astype(jnp.float32), None

        out_total, _ = lax.scan(add_block, jnp.zeros((TOK_DEV, D), jnp.float32), (hidden_blocks, weight_blocks))
        output = out_total.astype(jnp.bfloat16)
        hidden_grad = lax.dot_general(cot_rows, down_weight, (((1,), (1,)), ((), ())), preferred_element_type=jnp.float32)
        gate_grad = (hidden_grad * up_wide * sigmoid_gate * (1.0 + gate_wide * (1.0 - sigmoid_gate))).astype(jnp.bfloat16)
        up_grad = (hidden_grad * activation).astype(jnp.bfloat16)
        grad_term = lax.dot_general(hidden, cot_rows, (((0,), (0,)), ((), ())), preferred_element_type=jnp.float32) / N_DP
        rounded = lax.optimization_barrier(grad_term.astype(jnp.bfloat16))
        grad_total = grad_total + rounded.astype(jnp.float32)
        return grad_total, (output, gate_grad, up_grad)

    start_total = jnp.zeros((FF, D), jnp.float32)
    grad_total, (output, gate_grad, up_grad) = lax.scan(one_group, start_total, (gate_groups, up_groups, cot_groups))
    return (output.reshape(TOKENS, D), gate_grad.reshape(TOKENS, FF), up_grad.reshape(TOKENS, FF), grad_total.astype(jnp.bfloat16))
```

```python
import jax
import jax.numpy as jnp
from jax import lax
from jax.sharding import Mesh, PartitionSpec as P

NX, NYH, NC, NYL, NZ = 4, 4, 2, 2, 12
BF, F32 = jnp.bfloat16, jnp.float32


tie = lax.optimization_barrier


def shift(n, by):
    return [(i, (i + by) % n) for i in range(n)]


def per_device(gate_pre, up_pre, down_weight, cotangent):
    tok, ff = gate_pre.shape
    rows, feat = cotangent.shape
    half = feat // NC
    lane = half // (NX * NYH)
    core, yl, z = lax.axis_index("c"), lax.axis_index("yl"), lax.axis_index("z")

    def halves(array):
        blocks = [array[:, i * lane : (i + 1) * lane] for i in range(NX * NYH * NC)]
        return jnp.concatenate(blocks[0::2], axis=1), jnp.concatenate(blocks[1::2], axis=1)

    even, odd = halves(cotangent)
    mine = jnp.where(core == 0, even, odd)
    other = jnp.where(core == 0, odd, even)
    swap2 = [(0, 1), (1, 0)]
    diagonal = [(0, 3), (1, 2), (2, 1), (3, 0)]
    from_core = lax.ppermute(other, "c", swap2)
    from_yl = lax.ppermute(mine, "yl", swap2)
    from_diag = lax.ppermute(other, ("c", "yl"), diagonal)
    first = yl == 0
    block = jnp.concatenate(
        [
            jnp.where(first, mine, from_yl),
            jnp.where(first, from_yl, mine),
            jnp.where(first, from_core, from_diag),
            jnp.where(first, from_diag, from_core),
        ],
        axis=0,
    )

    gate_wide = gate_pre.astype(F32)
    up_wide = up_pre.astype(F32)
    sig = jax.nn.sigmoid(gate_wide)
    act = gate_wide * sig
    hidden, block = tie(((act * up_wide).astype(BF), block))
    hidden_z = hidden.reshape(NYL, NZ, rows, ff).transpose(1, 0, 2, 3).reshape(tok, ff)
    partial = jnp.dot(hidden_z, down_weight, preferred_element_type=F32).astype(BF)
    hidden_peer = lax.ppermute(hidden_z, "c", swap2)
    hidden_both = jnp.concatenate(
        [hidden_z.reshape(NZ, NYL * rows, ff), hidden_peer.reshape(NZ, NYL * rows, ff)], axis=1
    ).reshape(NC * tok, ff)

    w_even, w_odd = halves(down_weight)
    w_half = jnp.where(core == 0, w_even, w_odd)

    ring = jnp.zeros((NZ,) + block.shape, BF)
    put = lambda buf, piece, at: lax.dynamic_update_slice(
        buf, piece[None], (lax.rem(at + NZ, NZ), 0, 0)
    )
    ring = put(ring, block, z)
    up, down = block, block
    for step in range(1, NZ // 2 + 1):
        up = lax.ppermute(up, "z", shift(NZ, 1))
        ring = put(ring, up, z - step)
        if step < NZ // 2:
            down = lax.ppermute(down, "z", shift(NZ, -1))
            ring = put(ring, down, z + step)
        if step == 1:
            up, down, partial = tie((up, down, partial))
            out_z = lax.psum_scatter(partial, "z", scatter_dimension=0, tiled=True)
        if step == 2:
            up, down, hidden_both = tie((up, down, hidden_both))
        if step == 3:
            up, down, w_half = tie((up, down, w_half))
    cot_both = ring.reshape(NC * tok, half)

    grad_acc = lax.dot_general(
        cot_both, hidden_both, (((0,), (0,)), ((), ())), preferred_element_type=F32
    )
    term = (grad_acc / (NX * NYH * NC)).astype(BF).reshape(NX, half // NX, ff)
    term, cot_both, up_pre, gate_pre = tie((term, cot_both, up_pre, gate_pre))
    by_x = lax.all_to_all(term, "x", 0, 0)
    sum_x = by_x.astype(F32).sum(0).astype(BF).reshape(NYH, lane, ff)
    by_y = lax.all_to_all(sum_x, "yh", 0, 0)
    weight_grad = by_y.astype(F32).sum(0).astype(BF).T

    back_part = lax.dot_general(
        cot_both, w_half, (((1,), (1,)), ((), ())), preferred_element_type=F32
    ).reshape(NZ, NC, NYL * rows, ff)
    back_z = back_part[:, 0] + lax.ppermute(back_part[:, 1], "c", swap2)
    gate_wide = gate_pre.astype(F32)
    up_wide = up_pre.astype(F32)
    sig = jax.nn.sigmoid(gate_wide)
    act = gate_wide * sig
    back = back_z.reshape(NZ, NYL, rows, ff).transpose(1, 0, 2, 3).reshape(tok, ff)
    gate_grad = (back * up_wide * sig * (1.0 + gate_wide * (1.0 - sig))).astype(BF)
    up_grad = (back * act).astype(BF)

    keep = lax.dynamic_slice_in_dim(out_z, yl * rows, rows, 0)
    give = lax.dynamic_slice_in_dim(out_z, (1 - yl) * rows, rows, 0)
    got = lax.ppermute(give, "yl", swap2)
    output = (keep.astype(F32) + got.astype(F32)).astype(BF)
    return output, gate_grad, up_grad, weight_grad


def solution(mesh):
    fine = Mesh(
        mesh.devices.reshape(NX, NYH, NC, NYL, NZ), ("x", "yh", "c", "yl", "z")
    )
    dp, tensor = ("x", "yh", "c"), ("yl", "z")
    return jax.shard_map(
        per_device,
        mesh=fine,
        in_specs=(P(dp, tensor), P(dp, tensor), P(tensor, None), P(dp + tensor, None)),
        out_specs=(P(dp + tensor, None), P(dp, tensor), P(dp, tensor), P(tensor, dp)),
        check_vma=False,
    )
```

```python
import jax
import jax.numpy as jnp
from jax import lax
from jax.experimental import pallas as pl
from jax.experimental.pallas import tpu as pltpu
from jax.sharding import Mesh, PartitionSpec as P

NX, NYH, NC, NYL, NZ = 4, 4, 2, 2, 12
CHUNKS = 2
PER = NYH // CHUNKS
BF, F32 = jnp.bfloat16, jnp.float32
SWAP = [(0, 1), (1, 0)]
tie = lax.optimization_barrier


def source_block(slot):
    chunk, rest = slot // (NX * PER), slot % (NX * PER)
    return (rest // PER) * NYH + chunk * PER + rest % PER


def split_kernel(core_ref, cot_ref, mine_ref, other_ref):
    lane = mine_ref.shape[1] // (NX * NYH)
    zero = core_ref[0] == 0
    for slot in range(NX * NYH):
        at = source_block(slot) * NC * lane
        even = cot_ref[:, at : at + lane]
        odd = cot_ref[:, at + lane : at + NC * lane]
        mine_ref[:, slot * lane : (slot + 1) * lane] = jnp.where(zero, even, odd)
        other_ref[:, slot * lane : (slot + 1) * lane] = jnp.where(zero, odd, even)


def split_columns(core, cot):
    rows, feat = cot.shape
    shape = jax.ShapeDtypeStruct((rows, feat // NC), cot.dtype)
    return pl.pallas_call(
        split_kernel,
        out_shape=(shape, shape),
        in_specs=[
            pl.BlockSpec(memory_space=pltpu.SMEM),
            pl.BlockSpec(memory_space=pltpu.VMEM),
        ],
        out_specs=(pl.BlockSpec(memory_space=pltpu.VMEM),) * 2,
        name="split_columns",
    )(core.reshape(1), cot)


def half_kernel(core_ref, a_ref, b_ref, out_ref):
    lane = a_ref.shape[1]
    out_ref[:, :lane] = a_ref[...]
    out_ref[:, lane:] = b_ref[...]


def half_weight(core, weight):
    ff, feat = weight.shape
    lane = feat // (NX * NYH * NC)
    pick = lambda k: pl.BlockSpec(
        (ff, lane), lambda i, core_ref: (0, source_block(2 * i + k) * NC + core_ref[0])
    )
    return pl.pallas_call(
        half_kernel,
        out_shape=jax.ShapeDtypeStruct((ff, feat // NC), weight.dtype),
        grid_spec=pltpu.PrefetchScalarGridSpec(
            num_scalar_prefetch=1,
            grid=(NX * NYH // 2,),
            in_specs=[pick(0), pick(1)],
            out_specs=pl.BlockSpec((ff, 2 * lane), lambda i, core_ref: (0, i)),
        ),
        name="half_weight",
    )(core.reshape(1), weight, weight)


def per_device(gate_pre, up_pre, down_weight, cotangent):
    tok, ff = gate_pre.shape
    rows, feat = cotangent.shape
    half = feat // NC
    width = half // CHUNKS
    lane = half // (NX * NYH)
    core, yl = lax.axis_index("c"), lax.axis_index("yl")
    first = yl == 0

    mine, other = split_columns(core, cotangent)
    from_core = lax.ppermute(other, "c", SWAP)

    gate_wide = gate_pre.astype(F32)
    up_wide = up_pre.astype(F32)
    sig = jax.nn.sigmoid(gate_wide)
    act = gate_wide * sig
    hidden = (act * up_wide).astype(BF)
    hidden_z = hidden.reshape(NYL, NZ, rows, ff).transpose(1, 0, 2, 3)
    hidden_z, from_core = tie((hidden_z, from_core))
    partial = jnp.dot(hidden_z.reshape(tok, ff), down_weight, preferred_element_type=F32).astype(BF)
    partial, from_core, hidden_z = tie((partial, from_core, hidden_z))
    out_z = lax.psum_scatter(partial, "z", scatter_dimension=0, tiled=True)
    hidden_peer = lax.ppermute(hidden_z, "c", SWAP)

    shard = jnp.concatenate([mine, from_core], axis=0)
    w_half = half_weight(core, down_weight)
    own = [None] * CHUNKS
    theirs = [None] * CHUNKS
    for k in range(CHUNKS):
        piece = shard[:, k * width : (k + 1) * width]
        if k:
            piece, own[k - 1] = tie((piece, own[k - 1]))
        own[k] = lax.all_gather(piece, "z", axis=0, tiled=True)
        theirs[k] = lax.ppermute(own[k], "yl", SWAP)

    pair = jnp.stack([hidden_z, hidden_peer], axis=2)
    low, high = pair[:, 0], pair[:, 1]
    hidden_both = jnp.stack(
        [jnp.where(first, low, high), jnp.where(first, high, low)], axis=0
    ).reshape(NC * tok, ff)

    back_part = 0.0
    sums = []
    for k in range(CHUNKS):
        cot_k = jnp.concatenate([own[k], theirs[k]], axis=0)
        grad_acc = lax.dot_general(
            cot_k, hidden_both, (((0,), (0,)), ((), ())), preferred_element_type=F32
        )
        term = (grad_acc / (NX * NYH * NC)).astype(BF).reshape(NX, PER * lane, ff)
        term, cot_k, gate_pre, up_pre = tie((term, cot_k, gate_pre, up_pre))
        by_x = lax.all_to_all(term, "x", 0, 0)
        back_part = back_part + lax.dot_general(
            cot_k,
            w_half[:, k * width : (k + 1) * width],
            (((1,), (1,)), ((), ())),
            preferred_element_type=F32,
        )
        sums.append(by_x.astype(F32).sum(0).astype(BF).reshape(PER, lane, ff))
    by_y = lax.all_to_all(jnp.concatenate(sums, axis=0), "yh", 0, 0)
    weight_grad = by_y.astype(F32).sum(0).astype(BF).T

    back_part = back_part.reshape(NYL, NZ, NC, rows, ff)
    back = back_part[:, :, 0].reshape(tok, ff)
    back = back + lax.ppermute(back_part[:, :, 1].reshape(tok, ff), "c", SWAP)
    near, far = back[: tok // NYL], back[tok // NYL :]
    back = jnp.concatenate([jnp.where(first, near, far), jnp.where(first, far, near)], axis=0)
    gate_wide = gate_pre.astype(F32)
    up_wide = up_pre.astype(F32)
    sig = jax.nn.sigmoid(gate_wide)
    act = gate_wide * sig
    gate_grad = (back * up_wide * sig * (1.0 + gate_wide * (1.0 - sig))).astype(BF)
    up_grad = (back * act).astype(BF)

    keep = lax.dynamic_slice_in_dim(out_z, yl * rows, rows, 0)
    give = lax.dynamic_slice_in_dim(out_z, (1 - yl) * rows, rows, 0)
    got = lax.ppermute(give, "yl", SWAP)
    output = (keep.astype(F32) + got.astype(F32)).astype(BF)
    return output, gate_grad, up_grad, weight_grad


def solution(mesh):
    fine = Mesh(
        mesh.devices.reshape(NX, NYH, NC, NYL, NZ), ("x", "yh", "c", "yl", "z")
    )
    dp, tensor = ("x", "yh", "c"), ("yl", "z")
    return jax.shard_map(
        per_device,
        mesh=fine,
        in_specs=(P(dp, tensor), P(dp, tensor), P(tensor, None), P(dp + tensor, None)),
        out_specs=(P(dp + tensor, None), P(dp, tensor), P(dp, tensor), P(tensor, dp)),
        check_vma=False,
    )
```

```python
import jax
import jax.numpy as jnp
from jax import lax
from jax.experimental import pallas as pl
from jax.experimental.pallas import tpu as pltpu
from jax.sharding import Mesh, PartitionSpec as P

NX, NYH, NC, NYL, NZ = 4, 4, 2, 2, 12
LANES = (64, 64)
BF, F32 = jnp.bfloat16, jnp.float32
SWAP = [(0, 1), (1, 0)]
tie = lax.optimization_barrier


def pick_chunk(ref, half, lane, chunk):
    start = sum(LANES[:chunk])
    pieces = []
    for pair in range(NX * NYH):
        at = (pair * NC + half) * lane
        pieces.append(ref[:, at : at + lane][:, start : start + LANES[chunk]])
    return jnp.concatenate(pieces, axis=1)


def split_kernel(core_ref, cot_ref, *out_refs):
    lane = cot_ref.shape[1] // (NX * NYH * NC)
    mine_refs, other_refs = out_refs[: len(LANES)], out_refs[len(LANES) :]
    for core in range(NC):

        @pl.when(core_ref[0] == core)
        def _():
            for chunk in range(len(LANES)):
                mine_refs[chunk][...] = pick_chunk(cot_ref, core, lane, chunk)
                other_refs[chunk][...] = pick_chunk(cot_ref, 1 - core, lane, chunk)


def split_columns(core, cot):
    rows, feat = cot.shape
    shapes = [jax.ShapeDtypeStruct((rows, NX * NYH * n), cot.dtype) for n in LANES]
    vmem = pl.BlockSpec(memory_space=pltpu.VMEM)
    outs = pl.pallas_call(
        split_kernel,
        out_shape=shapes * 2,
        in_specs=[pl.BlockSpec(memory_space=pltpu.SMEM), vmem],
        out_specs=[vmem] * (2 * len(LANES)),
        name="split_columns",
    )(core.reshape(1), cot)
    return outs[: len(LANES)], outs[len(LANES) :]


def half_kernel(core_ref, weight_ref, *out_refs):
    lane = weight_ref.shape[1] // (NX * NYH * NC)
    for core in range(NC):

        @pl.when(core_ref[0] == core)
        def _():
            for chunk, out_ref in enumerate(out_refs):
                out_ref[...] = pick_chunk(weight_ref, core, lane, chunk)


def half_weight(core, weight):
    ff, feat = weight.shape
    step = 128
    return pl.pallas_call(
        half_kernel,
        out_shape=[jax.ShapeDtypeStruct((ff, NX * NYH * n), weight.dtype) for n in LANES],
        grid=(ff // step,),
        in_specs=[
            pl.BlockSpec(memory_space=pltpu.SMEM),
            pl.BlockSpec((step, feat), lambda i: (i, 0)),
        ],
        out_specs=[pl.BlockSpec((step, NX * NYH * n), lambda i: (i, 0)) for n in LANES],
        name="half_weight",
    )(core.reshape(1), weight)


def scatter_sum(terms, axis):
    size = terms.shape[0]
    me = lax.axis_index(axis)
    total = lax.dynamic_index_in_dim(terms, me, 0, False).astype(F32)
    for by in (1, size - 1, 2):
        to = lax.rem(me + by, size)
        pairs = [(i, (i + by) % size) for i in range(size)]
        piece = lax.dynamic_index_in_dim(terms, to, 0, False)
        total = total + lax.ppermute(piece, axis, pairs).astype(F32)
    return total.astype(BF)


def per_device(gate_pre, up_pre, down_weight, cotangent):
    tok, ff = gate_pre.shape
    rows, feat = cotangent.shape
    core, yl = lax.axis_index("c"), lax.axis_index("yl")
    first = yl == 0
    part = tok // NYL

    mine, other = split_columns(core, cotangent)
    from_core = lax.ppermute(jnp.concatenate(other, axis=1), "c", SWAP)

    gate_wide = gate_pre.astype(F32)
    up_wide = up_pre.astype(F32)
    sig = jax.nn.sigmoid(gate_wide)
    act = gate_wide * sig
    hidden = (act * up_wide).astype(BF)
    hidden, from_core = tie((hidden, from_core))
    partial = jnp.dot(hidden, down_weight, preferred_element_type=F32).astype(BF)
    partial, from_core, hidden = tie((partial, from_core, hidden))
    keep = lax.dynamic_slice_in_dim(partial, yl * part, part, 0)
    give = lax.dynamic_slice_in_dim(partial, (1 - yl) * part, part, 0)
    got = lax.ppermute(give, "yl", SWAP)
    hidden_peer = lax.ppermute(hidden, "c", SWAP)

    own, theirs = [], []
    for k, n in enumerate(LANES):
        start = NX * NYH * sum(LANES[:k])
        piece = jnp.concatenate([mine[k], from_core[:, start : start + NX * NYH * n]], axis=0)
        if k == 1:
            kept = (keep.astype(F32) + got.astype(F32)).astype(BF).reshape(NZ, rows, feat)
            piece, kept, own[0] = tie((piece, kept, own[0]))
            by_z = lax.all_to_all(kept, "z", 0, 0)
        elif k:
            piece, own[k - 1] = tie((piece, own[k - 1]))
        own.append(lax.all_gather(piece, "z", axis=0, tiled=True))
        theirs.append(lax.ppermute(own[k], "yl", SWAP))
    w_half = half_weight(core, down_weight)

    pair = jnp.stack([hidden, hidden_peer]).reshape(NC, NYL, NZ, rows, ff).transpose(1, 2, 0, 3, 4)
    hidden_both = jnp.stack(
        [jnp.where(first, pair[0], pair[1]), jnp.where(first, pair[1], pair[0])]
    ).reshape(NC * tok, ff)

    back_part = 0.0
    grads = []
    for k, n in enumerate(LANES):
        cot_k = jnp.concatenate([own[k], theirs[k]], axis=0)
        grad_acc = lax.dot_general(
            cot_k, hidden_both, (((0,), (0,)), ((), ())), preferred_element_type=F32
        )
        term = (grad_acc / (NX * NYH * NC)).astype(BF).reshape(NX, NYH * n, ff)
        term, cot_k, gate_pre, up_pre = tie((term, cot_k, gate_pre, up_pre))
        if k < len(LANES) - 1:
            sum_x = scatter_sum(term, "x")
        else:
            term, by_z = tie((term, by_z))
            sum_x = lax.all_to_all(term, "x", 0, 0).astype(F32).sum(0).astype(BF)
        back_part = back_part + lax.dot_general(
            cot_k, w_half[k], (((1,), (1,)), ((), ())), preferred_element_type=F32
        )
        sum_x = sum_x.reshape(NYH, n, ff)
        if k < len(LANES) - 1:
            grads.append(scatter_sum(sum_x, "yh"))
        else:
            grads.append(lax.all_to_all(sum_x, "yh", 0, 0).astype(F32).sum(0).astype(BF))
    weight_grad = jnp.concatenate(grads, axis=0).T

    output = by_z.astype(F32).sum(0).astype(BF)

    back_part = back_part.reshape(NYL, NZ, NC, rows, ff)
    back = back_part[:, :, 0].reshape(tok, ff)
    back = back + lax.ppermute(back_part[:, :, 1].reshape(tok, ff), "c", SWAP)
    near, far = back[: tok // NYL], back[tok // NYL :]
    back = jnp.concatenate([jnp.where(first, near, far), jnp.where(first, far, near)], axis=0)
    gate_wide = gate_pre.astype(F32)
    up_wide = up_pre.astype(F32)
    sig = jax.nn.sigmoid(gate_wide)
    act = gate_wide * sig
    gate_grad = (back * up_wide * sig * (1.0 + gate_wide * (1.0 - sig))).astype(BF)
    up_grad = (back * act).astype(BF)

    return output, gate_grad, up_grad, weight_grad


def solution(mesh):
    fine = Mesh(
        mesh.devices.reshape(NX, NYH, NC, NYL, NZ), ("x", "yh", "c", "yl", "z")
    )
    dp, tensor = ("x", "yh", "c"), ("yl", "z")
    return jax.shard_map(
        per_device,
        mesh=fine,
        in_specs=(P(dp, tensor), P(dp, tensor), P(tensor, None), P(dp + tensor, None)),
        out_specs=(P(dp + tensor, None), P(dp, tensor), P(dp, tensor), P(tensor, dp)),
        check_vma=False,
    )
```

```python
import jax
import jax.numpy as jnp
from jax import lax
from jax.experimental import pallas as pl
from jax.experimental.pallas import tpu as pltpu
from jax.sharding import Mesh, PartitionSpec as P

NX, NYH, NC, NYL, NZ = 4, 4, 2, 2, 12
CHUNKS = 2
GATHERED = 14
PER = NYH // CHUNKS
BF, F32 = jnp.bfloat16, jnp.float32
SWAP = [(0, 1), (1, 0)]
tie = lax.optimization_barrier


def source_block(slot):
    chunk, rest = slot // (NX * PER), slot % (NX * PER)
    return (rest // PER) * NYH + chunk * PER + rest % PER


def copy_half(out_ref, ref, half):
    lane = out_ref.shape[1] // (NX * NYH)
    for slot in range(NX * NYH):
        at = (source_block(slot) * NC + half) * lane
        out_ref[:, slot * lane : (slot + 1) * lane] = ref[:, at : at + lane]


def split_kernel(core_ref, cot_ref, mine_ref, other_ref):
    for core in range(NC):

        @pl.when(core_ref[0] == core)
        def _():
            copy_half(mine_ref, cot_ref, core)
            copy_half(other_ref, cot_ref, 1 - core)


def split_columns(core, cot):
    rows, feat = cot.shape
    shape = jax.ShapeDtypeStruct((rows, feat // NC), cot.dtype)
    return pl.pallas_call(
        split_kernel,
        out_shape=(shape, shape),
        in_specs=[
            pl.BlockSpec(memory_space=pltpu.SMEM),
            pl.BlockSpec(memory_space=pltpu.VMEM),
        ],
        out_specs=(pl.BlockSpec(memory_space=pltpu.VMEM),) * 2,
        name="split_columns",
    )(core.reshape(1), cot)


def half_kernel(core_ref, weight_ref, out_ref):
    for core in range(NC):

        @pl.when(core_ref[0] == core)
        def _():
            copy_half(out_ref, weight_ref, core)


def half_weight(core, weight):
    ff, feat = weight.shape
    step = 128
    return pl.pallas_call(
        half_kernel,
        out_shape=jax.ShapeDtypeStruct((ff, feat // NC), weight.dtype),
        grid=(ff // step,),
        in_specs=[
            pl.BlockSpec(memory_space=pltpu.SMEM),
            pl.BlockSpec((step, feat), lambda i: (i, 0)),
        ],
        out_specs=pl.BlockSpec((step, feat // NC), lambda i: (i, 0)),
        name="half_weight",
    )(core.reshape(1), weight)


def per_device(gate_pre, up_pre, down_weight, cotangent):
    tok, ff = gate_pre.shape
    rows, feat = cotangent.shape
    half = feat // NC
    width = half // CHUNKS
    lane = half // (NX * NYH)
    core, yl = lax.axis_index("c"), lax.axis_index("yl")
    first = yl == 0

    mine, other = split_columns(core, cotangent)
    from_core = lax.ppermute(other, "c", SWAP)

    gate_wide = gate_pre.astype(F32)
    up_wide = up_pre.astype(F32)
    sig = jax.nn.sigmoid(gate_wide)
    act = gate_wide * sig
    hidden = (act * up_wide).astype(BF)
    hidden_z = hidden.reshape(NYL, NZ, rows, ff).transpose(1, 0, 2, 3)
    hidden_z, from_core = tie((hidden_z, from_core))
    partial = jnp.dot(hidden_z.reshape(tok, ff), down_weight, preferred_element_type=F32).astype(BF)
    partial, from_core, hidden_z = tie((partial, from_core, hidden_z))
    out_z = lax.psum_scatter(partial, "z", scatter_dimension=0, tiled=True)
    hidden_peer = lax.ppermute(hidden_z, "c", SWAP)

    shard = jnp.concatenate([mine, from_core], axis=0)
    main, rest = shard[:, : GATHERED * lane], shard[:, GATHERED * lane :]
    rest = jnp.broadcast_to(rest[None], (NZ,) + rest.shape)
    main, rest = tie((main, rest))
    rest_all = lax.all_to_all(rest, "z", 0, 0).reshape(tok, -1)
    main_all = lax.all_gather(main, "z", axis=0, tiled=True)
    own = [main_all[:, :width], jnp.concatenate([main_all[:, width:], rest_all], axis=1)]
    theirs = [lax.ppermute(rows_k, "yl", SWAP) for rows_k in own]
    weight, main_all = tie((down_weight, main_all))
    w_half = half_weight(core, weight)

    pair = jnp.stack([hidden_z, hidden_peer], axis=2)
    low, high = pair[:, 0], pair[:, 1]
    hidden_both = jnp.stack(
        [jnp.where(first, low, high), jnp.where(first, high, low)], axis=0
    ).reshape(NC * tok, ff)

    back_part = 0.0
    sums = []
    for k in range(CHUNKS):
        cot_k = jnp.concatenate([own[k], theirs[k]], axis=0)
        grad_acc = lax.dot_general(
            cot_k, hidden_both, (((0,), (0,)), ((), ())), preferred_element_type=F32
        )
        term = (grad_acc / (NX * NYH * NC)).astype(BF).reshape(NX, PER * lane, ff)
        term, cot_k, gate_pre, up_pre = tie((term, cot_k, gate_pre, up_pre))
        by_x = lax.all_to_all(term, "x", 0, 0)
        back_part = back_part + lax.dot_general(
            cot_k,
            w_half[:, k * width : (k + 1) * width],
            (((1,), (1,)), ((), ())),
            preferred_element_type=F32,
        )
        sums.append(by_x.astype(F32).sum(0).astype(BF).reshape(PER, lane, ff))
    by_y = lax.all_to_all(jnp.concatenate(sums, axis=0), "yh", 0, 0)
    weight_grad = by_y.astype(F32).sum(0).astype(BF).T

    back_part = back_part.reshape(NYL, NZ, NC, rows, ff)
    back = back_part[:, :, 0].reshape(tok, ff)
    back = back + lax.ppermute(back_part[:, :, 1].reshape(tok, ff), "c", SWAP)
    near, far = back[: tok // NYL], back[tok // NYL :]
    back = jnp.concatenate([jnp.where(first, near, far), jnp.where(first, far, near)], axis=0)
    gate_wide = gate_pre.astype(F32)
    up_wide = up_pre.astype(F32)
    sig = jax.nn.sigmoid(gate_wide)
    act = gate_wide * sig
    gate_grad = (back * up_wide * sig * (1.0 + gate_wide * (1.0 - sig))).astype(BF)
    up_grad = (back * act).astype(BF)

    keep = lax.dynamic_slice_in_dim(out_z, yl * rows, rows, 0)
    give = lax.dynamic_slice_in_dim(out_z, (1 - yl) * rows, rows, 0)
    got = lax.ppermute(give, "yl", SWAP)
    output = (keep.astype(F32) + got.astype(F32)).astype(BF)
    return output, gate_grad, up_grad, weight_grad


def solution(mesh):
    fine = Mesh(
        mesh.devices.reshape(NX, NYH, NC, NYL, NZ), ("x", "yh", "c", "yl", "z")
    )
    dp, tensor = ("x", "yh", "c"), ("yl", "z")
    return jax.shard_map(
        per_device,
        mesh=fine,
        in_specs=(P(dp, tensor), P(dp, tensor), P(tensor, None), P(dp + tensor, None)),
        out_specs=(P(dp + tensor, None), P(dp, tensor), P(dp, tensor), P(tensor, dp)),
        check_vma=False,
    )
```

```python
import functools

import jax
import jax.numpy as jnp
from jax import lax
from jax.experimental import pallas as pl
from jax.experimental.pallas import tpu as pltpu
from jax.sharding import Mesh, PartitionSpec as P

NX, NYH, NC, NYL, NZ = 4, 4, 2, 2, 12
GATHERED = 14
BF, F32 = jnp.bfloat16, jnp.float32
SWAP = [(0, 1), (1, 0)]
tie = lax.optimization_barrier


def copy_half(out_ref, ref, half):
    lane = out_ref.shape[1] // (NX * NYH)
    for slot in range(NX * NYH):
        at = (slot * NC + half) * lane
        out_ref[:, slot * lane : (slot + 1) * lane] = ref[:, at : at + lane]


def split_kernel(core_ref, cot_ref, mine_ref, other_ref):
    for core in range(NC):

        @pl.when(core_ref[0] == core)
        def _():
            copy_half(mine_ref, cot_ref, core)
            copy_half(other_ref, cot_ref, 1 - core)


def split_columns(core, cot):
    rows, feat = cot.shape
    shape = jax.ShapeDtypeStruct((rows, feat // NC), cot.dtype)
    return pl.pallas_call(
        split_kernel,
        out_shape=(shape, shape),
        in_specs=[
            pl.BlockSpec(memory_space=pltpu.SMEM),
            pl.BlockSpec(memory_space=pltpu.VMEM),
        ],
        out_specs=(pl.BlockSpec(memory_space=pltpu.VMEM),) * 2,
        name="split_columns",
    )(core.reshape(1), cot)


def half_kernel(core_ref, weight_ref, out_ref):
    for core in range(NC):

        @pl.when(core_ref[0] == core)
        def _():
            copy_half(out_ref, weight_ref, core)


def half_weight(core, weight):
    ff, feat = weight.shape
    step = 128
    return pl.pallas_call(
        half_kernel,
        out_shape=jax.ShapeDtypeStruct((ff, feat // NC), weight.dtype),
        grid=(ff // step,),
        in_specs=[
            pl.BlockSpec(memory_space=pltpu.SMEM),
            pl.BlockSpec((step, feat), lambda i: (i, 0)),
        ],
        out_specs=pl.BlockSpec((step, feat // NC), lambda i: (i, 0)),
        name="half_weight",
    )(core.reshape(1), weight)


def grad_kernel(scale, *refs):
    main_near, rest_near, main_far, rest_far, hidden_near, hidden_far, out_ref = refs

    def product(near, far):
        turned = (((0,), (0,)), ((), ()))
        acc = lax.dot_general(near[...], hidden_near[...], turned, preferred_element_type=F32)
        acc += lax.dot_general(far[...], hidden_far[...], turned, preferred_element_type=F32)
        out_ref[...] = (acc * scale).astype(out_ref.dtype)

    last = pl.program_id(0) == pl.num_programs(0) - 1

    @pl.when(jnp.logical_not(last))
    def _():
        product(main_near, main_far)

    @pl.when(last)
    def _():
        product(rest_near, rest_far)


def weight_term(scale, main_near, rest_near, main_far, rest_far, hidden_near, hidden_far):
    tok, ff = hidden_near.shape
    width = rest_near.shape[1]
    blocks = main_near.shape[1] // width
    main = pl.BlockSpec((tok, width), lambda i: (0, jnp.minimum(i, blocks - 1)))
    rest = pl.BlockSpec((tok, width), lambda i: (0, 0))
    whole = pl.BlockSpec((tok, ff), lambda i: (0, 0))
    return pl.pallas_call(
        functools.partial(grad_kernel, scale),
        out_shape=jax.ShapeDtypeStruct(((blocks + 1) * width, ff), BF),
        grid=(blocks + 1,),
        in_specs=[main, rest, main, rest, whole, whole],
        out_specs=pl.BlockSpec((width, ff), lambda i: (i, 0)),
        name="weight_term",
    )(main_near, rest_near, main_far, rest_far, hidden_near, hidden_far)


def per_device(gate_pre, up_pre, down_weight, cotangent):
    tok, ff = gate_pre.shape
    rows, feat = cotangent.shape
    half = feat // NC
    lane = half // (NX * NYH)
    core, yl = lax.axis_index("c"), lax.axis_index("yl")
    first = yl == 0
    part = tok // NYL
    across = (((1,), (1,)), ((), ()))

    mine, other = split_columns(core, cotangent)
    from_core = lax.ppermute(other, "c", SWAP)
    gate_wide = gate_pre.astype(F32)
    up_wide = up_pre.astype(F32)
    sig = jax.nn.sigmoid(gate_wide)
    act = gate_wide * sig
    hidden = (act * up_wide).astype(BF)
    hidden, from_core = tie((hidden, from_core))
    hidden_peer = lax.ppermute(hidden, "c", SWAP)

    shard = jnp.concatenate([mine, from_core], axis=0)
    main, rest = shard[:, : GATHERED * lane], shard[:, GATHERED * lane :]
    main_all = lax.all_gather(main, "z", axis=0, tiled=True)
    main_all, rest = tie((main_all, rest))
    main_far = lax.ppermute(main_all, "yl", SWAP)

    rest_all = lax.all_gather(rest, "z", axis=0, tiled=True)
    rest_all, hidden, hidden_peer = tie((rest_all, hidden, hidden_peer))
    rest_far = lax.ppermute(rest_all, "yl", SWAP)
    hidden_z = hidden.reshape(NYL, NZ, rows, ff).transpose(1, 0, 2, 3).reshape(tok, ff)
    partial = jnp.dot(hidden_z, down_weight, preferred_element_type=F32).astype(BF)
    partial, hidden, hidden_peer = tie((partial, hidden, hidden_peer))
    out_z = lax.psum_scatter(partial, "z", scatter_dimension=0, tiled=True)

    def gathered_order(at):
        both = [lax.dynamic_slice_in_dim(h, at * part, part, 0) for h in (hidden, hidden_peer)]
        return jnp.stack([h.reshape(NZ, rows, ff) for h in both], axis=1).reshape(tok, ff)

    hidden_near, hidden_far = gathered_order(yl), gathered_order(1 - yl)
    main_far, rest_far, hidden_near, hidden_far = tie(
        (main_far, rest_far, hidden_near, hidden_far)
    )

    scale = 1.0 / (NX * NYH * NC)
    term = weight_term(scale, main_all, rest_all, main_far, rest_far, hidden_near, hidden_far)
    term = term.reshape(NX, NYH * lane, ff)
    term, main_all, main_far, gate_pre, up_pre, weight = tie(
        (term, main_all, main_far, gate_pre, up_pre, down_weight)
    )
    by_x = lax.all_to_all(term, "x", 0, 0)

    w_half = half_weight(core, weight)
    back_near, back_far = [
        lax.dot_general(
            jnp.concatenate(c, axis=1), w_half, across, preferred_element_type=F32
        ).reshape(NZ, NC, rows, ff)
        for c in ((main_all, rest_all), (main_far, rest_far))
    ]

    def rows_of(which):
        ordered = [back_near[:, which], back_far[:, which]]
        low, high = [b.reshape(part, ff) for b in ordered]
        return jnp.concatenate([jnp.where(first, low, high), jnp.where(first, high, low)], axis=0)

    back = rows_of(0) + lax.ppermute(rows_of(1), "c", SWAP)
    gate_wide = gate_pre.astype(F32)
    up_wide = up_pre.astype(F32)
    sig = jax.nn.sigmoid(gate_wide)
    act = gate_wide * sig
    gate_grad = (back * up_wide * sig * (1.0 + gate_wide * (1.0 - sig))).astype(BF)
    up_grad = (back * act).astype(BF)

    sum_x = by_x.astype(F32).sum(0).astype(BF).reshape(NYH, lane, ff)
    by_y = lax.all_to_all(sum_x, "yh", 0, 0)
    weight_grad = by_y.astype(F32).sum(0).astype(BF).T

    keep = lax.dynamic_slice_in_dim(out_z, yl * rows, rows, 0)
    give = lax.dynamic_slice_in_dim(out_z, (1 - yl) * rows, rows, 0)
    got = lax.ppermute(give, "yl", SWAP)
    output = (keep.astype(F32) + got.astype(F32)).astype(BF)
    return output, gate_grad, up_grad, weight_grad


def solution(mesh):
    fine = Mesh(
        mesh.devices.reshape(NX, NYH, NC, NYL, NZ), ("x", "yh", "c", "yl", "z")
    )
    dp, tensor = ("x", "yh", "c"), ("yl", "z")
    return jax.shard_map(
        per_device,
        mesh=fine,
        in_specs=(P(dp, tensor), P(dp, tensor), P(tensor, None), P(dp + tensor, None)),
        out_specs=(P(dp + tensor, None), P(dp, tensor), P(dp, tensor), P(tensor, dp)),
        check_vma=False,
    )
```

```python
import jax
import jax.numpy as jnp
from jax import lax
from jax.experimental import pallas as pl
from jax.experimental.pallas import tpu as pltpu
from jax.sharding import Mesh, PartitionSpec as P

NX, NYH, NC, NYL, NZ = 4, 4, 2, 2, 12
NB = NX * NYH
GATHERED = 14
BF, F32 = jnp.bfloat16, jnp.float32
SWAP = [(0, 1), (1, 0)]
DIAGONAL = [(0, 3), (1, 2), (2, 1), (3, 0)]
tie = lax.optimization_barrier


def quarter(ref, core, yl):
    lane = ref.shape[1] // (NB * NC)
    half = lane // NYL
    pieces = []
    for pair in range(NB):
        at = (pair * NC + core) * lane
        pieces.append(ref[:, at : at + lane][:, yl * half : (yl + 1) * half])
    return jnp.concatenate(pieces, axis=1)


def split_kernel(place_ref, cot_ref, *out_refs):
    for core in range(NC):
        for yl in range(NYL):

            @pl.when(place_ref[0] == core * NYL + yl)
            def _():
                wanted = ((core, yl), (1 - core, yl), (core, 1 - yl), (1 - core, 1 - yl))
                for out_ref, (c, y) in zip(out_refs, wanted):
                    out_ref[...] = quarter(cot_ref, c, y)


def split_columns(place, cot):
    rows, feat = cot.shape
    vmem = pl.BlockSpec(memory_space=pltpu.VMEM)
    return pl.pallas_call(
        split_kernel,
        out_shape=[jax.ShapeDtypeStruct((rows, feat // 4), cot.dtype)] * 4,
        in_specs=[pl.BlockSpec(memory_space=pltpu.SMEM), vmem],
        out_specs=[vmem] * 4,
        name="split_columns",
    )(place, cot)


def weight_kernel(place_ref, weight_ref, near_ref, far_ref):
    for core in range(NC):
        for yl in range(NYL):

            @pl.when(place_ref[0] == core * NYL + yl)
            def _():
                near_ref[...] = quarter(weight_ref, core, yl)
                far_ref[...] = quarter(weight_ref, core, 1 - yl)


def weight_quarters(place, weight):
    ff, feat = weight.shape
    step = 128
    return pl.pallas_call(
        weight_kernel,
        out_shape=[jax.ShapeDtypeStruct((ff, feat // 4), weight.dtype)] * 2,
        grid=(ff // step,),
        in_specs=[
            pl.BlockSpec(memory_space=pltpu.SMEM),
            pl.BlockSpec((step, feat), lambda i: (i, 0)),
        ],
        out_specs=[pl.BlockSpec((step, feat // 4), lambda i: (i, 0))] * 2,
        name="weight_quarters",
    )(place, weight)


def per_device(gate_pre, up_pre, down_weight, cotangent):
    tok, ff = gate_pre.shape
    rows, feat = cotangent.shape
    block = feat // (NB * NC)
    half = block // NYL
    both = NYL * rows
    core, yl = lax.axis_index("c"), lax.axis_index("yl")
    first = yl == 0
    place = (core * NYL + yl).reshape(1)
    across = (((1,), (1,)), ((), ()))

    mine, to_core, to_yl, to_diag = split_columns(place, cotangent)
    from_core = lax.ppermute(to_core, "c", SWAP)
    from_yl = lax.ppermute(to_yl, "yl", SWAP)
    from_diag = lax.ppermute(to_diag, ("c", "yl"), DIAGONAL)

    gate_wide = gate_pre.astype(F32)
    up_wide = up_pre.astype(F32)
    sig = jax.nn.sigmoid(gate_wide)
    act = gate_wide * sig
    hidden = (act * up_wide).astype(BF)
    hidden_z = hidden.reshape(NYL, NZ, rows, ff).transpose(1, 0, 2, 3).reshape(tok, ff)
    hidden_z, from_core, from_yl, from_diag = tie((hidden_z, from_core, from_yl, from_diag))
    hidden_core = lax.ppermute(hidden_z, "c", SWAP)
    hidden_yl = lax.ppermute(hidden_z, "yl", SWAP)
    hidden_diag = lax.ppermute(hidden_z, ("c", "yl"), DIAGONAL)
    partial = jnp.dot(hidden_z, down_weight, preferred_element_type=F32).astype(BF)

    shard = jnp.concatenate(
        [
            jnp.where(first, mine, from_yl),
            jnp.where(first, from_yl, mine),
            jnp.where(first, from_core, from_diag),
            jnp.where(first, from_diag, from_core),
        ],
        axis=0,
    )
    main, rest = shard[:, : GATHERED * half], shard[:, GATHERED * half :]
    rest = jnp.broadcast_to(rest[None], (NZ,) + rest.shape)
    main, rest, partial = tie((main, rest, partial))
    out_z = lax.psum_scatter(partial, "z", scatter_dimension=0, tiled=True)
    rest_all = lax.all_to_all(rest, "z", 0, 0).reshape(NC * tok, -1)
    main_all = lax.all_gather(main, "z", axis=0, tiled=True)
    near = jnp.concatenate([main_all, rest_all], axis=1)
    near, hidden_core, hidden_yl, hidden_diag = tie((near, hidden_core, hidden_yl, hidden_diag))

    def stacked(a, b):
        return jnp.stack([a.reshape(NZ, both, ff), b.reshape(NZ, both, ff)], axis=1)

    hidden_all = jnp.concatenate(
        [stacked(hidden_z, hidden_core), stacked(hidden_yl, hidden_diag)], axis=-1
    ).reshape(NC * tok, NYL * ff)

    grad_acc = lax.dot_general(
        near, hidden_all, (((0,), (0,)), ((), ())), preferred_element_type=F32
    )
    term = (grad_acc / (NX * NYH * NC)).astype(BF).reshape(NX, NYH * half, NYL * ff)
    term, near, gate_pre, up_pre, weight = tie((term, near, gate_pre, up_pre, down_weight))
    by_x = lax.all_to_all(term, "x", 0, 0)

    far = lax.ppermute(near, "yl", SWAP)
    weight_near, weight_far = weight_quarters(place, weight)
    back = lax.dot_general(near, weight_near, across, preferred_element_type=F32)
    back = back + lax.dot_general(far, weight_far, across, preferred_element_type=F32)
    back = back.reshape(NZ, NC, both, ff)
    back_z = back[:, 0] + lax.ppermute(back[:, 1], "c", SWAP)
    back = back_z.reshape(NZ, NYL, rows, ff).transpose(1, 0, 2, 3).reshape(tok, ff)
    gate_wide = gate_pre.astype(F32)
    up_wide = up_pre.astype(F32)
    sig = jax.nn.sigmoid(gate_wide)
    act = gate_wide * sig
    gate_grad = (back * up_wide * sig * (1.0 + gate_wide * (1.0 - sig))).astype(BF)
    up_grad = (back * act).astype(BF)

    sum_x = by_x.astype(F32).sum(0).astype(BF).reshape(NYH, half, NYL, ff)
    own, other = sum_x[:, :, 0], sum_x[:, :, 1]
    sum_x = jnp.stack([jnp.where(first, own, other), jnp.where(first, other, own)], axis=1)
    by_y = lax.all_to_all(sum_x.reshape(NYH * NYL, half, ff), ("yh", "yl"), 0, 0)
    by_y = by_y.reshape(NYH, NYL * half, ff)
    weight_grad = by_y.astype(F32).sum(0).astype(BF).T

    keep = lax.dynamic_slice_in_dim(out_z, yl * rows, rows, 0)
    give = lax.dynamic_slice_in_dim(out_z, (1 - yl) * rows, rows, 0)
    got = lax.ppermute(give, "yl", SWAP)
    output = (keep.astype(F32) + got.astype(F32)).astype(BF)
    return output, gate_grad, up_grad, weight_grad


def solution(mesh):
    fine = Mesh(
        mesh.devices.reshape(NX, NYH, NC, NYL, NZ), ("x", "yh", "c", "yl", "z")
    )
    dp, tensor = ("x", "yh", "c"), ("yl", "z")
    return jax.shard_map(
        per_device,
        mesh=fine,
        in_specs=(P(dp, tensor), P(dp, tensor), P(tensor, None), P(dp + tensor, None)),
        out_specs=(P(dp + tensor, None), P(dp, tensor), P(dp, tensor), P(tensor, dp)),
        check_vma=False,
    )
```

```python
import jax
import jax.numpy as jnp
from jax import lax
from jax.experimental import pallas as pl
from jax.experimental.pallas import tpu as pltpu
from jax.sharding import Mesh, PartitionSpec as P

NX, NYH, NC, NYL, NZH, NZL = 4, 4, 2, 2, 6, 2
NZ = NZH * NZL
NB = NX * NYH
BF, F32 = jnp.bfloat16, jnp.float32
SWAP = [(0, 1), (1, 0)]
DIAGONAL = [(0, 3), (1, 2), (2, 1), (3, 0)]
tie = lax.optimization_barrier


def quarter(ref, core, yl):
    lane = ref.shape[1] // (NB * NC)
    half = lane // NYL
    pieces = []
    for pair in range(NB):
        at = (pair * NC + core) * lane
        pieces.append(ref[:, at : at + lane][:, yl * half : (yl + 1) * half])
    return jnp.concatenate(pieces, axis=1)


def split_kernel(place_ref, cot_ref, *out_refs):
    for core in range(NC):
        for yl in range(NYL):

            @pl.when(place_ref[0] == core * NYL + yl)
            def _():
                wanted = ((core, yl), (1 - core, yl), (core, 1 - yl), (1 - core, 1 - yl))
                for out_ref, (c, y) in zip(out_refs, wanted):
                    out_ref[...] = quarter(cot_ref, c, y)


def split_columns(place, cot):
    rows, feat = cot.shape
    vmem = pl.BlockSpec(memory_space=pltpu.VMEM)
    return pl.pallas_call(
        split_kernel,
        out_shape=[jax.ShapeDtypeStruct((rows, feat // 4), cot.dtype)] * 4,
        in_specs=[pl.BlockSpec(memory_space=pltpu.SMEM), vmem],
        out_specs=[vmem] * 4,
        name="split_columns",
    )(place, cot)


def weight_kernel(place_ref, weight_ref, near_ref, far_ref):
    for core in range(NC):
        for yl in range(NYL):

            @pl.when(place_ref[0] == core * NYL + yl)
            def _():
                near_ref[...] = quarter(weight_ref, core, yl)
                far_ref[...] = quarter(weight_ref, core, 1 - yl)


def weight_quarters(place, weight):
    ff, feat = weight.shape
    step = 128
    return pl.pallas_call(
        weight_kernel,
        out_shape=[jax.ShapeDtypeStruct((ff, feat // 4), weight.dtype)] * 2,
        grid=(ff // step,),
        in_specs=[
            pl.BlockSpec(memory_space=pltpu.SMEM),
            pl.BlockSpec((step, feat), lambda i: (i, 0)),
        ],
        out_specs=[pl.BlockSpec((step, feat // 4), lambda i: (i, 0))] * 2,
        name="weight_quarters",
    )(place, weight)


def per_device(gate_pre, up_pre, down_weight, cotangent):
    tok, ff = gate_pre.shape
    rows, feat = cotangent.shape
    block = feat // (NB * NC)
    half = block // NYL
    both = NYL * rows
    core, yl = lax.axis_index("c"), lax.axis_index("yl")
    first = yl == 0
    place = (core * NYL + yl).reshape(1)
    across = (((1,), (1,)), ((), ()))

    mine, to_core, to_yl, to_diag = split_columns(place, cotangent)
    from_core = lax.ppermute(to_core, "c", SWAP)
    from_yl = lax.ppermute(to_yl, "yl", SWAP)
    from_diag = lax.ppermute(to_diag, ("c", "yl"), DIAGONAL)

    gate_wide = gate_pre.astype(F32)
    up_wide = up_pre.astype(F32)
    sig = jax.nn.sigmoid(gate_wide)
    act = gate_wide * sig
    hidden = (act * up_wide).astype(BF)
    hidden_z = hidden.reshape(NYL, NZ, rows, ff).transpose(1, 0, 2, 3).reshape(tok, ff)
    hidden_z, from_core, from_yl, from_diag = tie((hidden_z, from_core, from_yl, from_diag))
    hidden_core = lax.ppermute(hidden_z, "c", SWAP)

    shard = jnp.concatenate(
        [
            jnp.where(first, mine, from_yl),
            jnp.where(first, from_yl, mine),
            jnp.where(first, from_core, from_diag),
            jnp.where(first, from_diag, from_core),
        ],
        axis=0,
    )
    hidden_near = jnp.stack([h.reshape(NZ, both, ff) for h in (hidden_z, hidden_core)], axis=1)
    shard, hidden_near, hidden_z = tie((shard, hidden_near, hidden_z))
    hidden_far = lax.ppermute(hidden_near.reshape(NC * tok, ff), "yl", SWAP)
    mine_z = lax.all_gather(shard, "zh", axis=0, tiled=True)
    mine_z, hidden_z, hidden_far = tie((mine_z, hidden_z, hidden_far))
    other_z = lax.ppermute(mine_z, "zl", SWAP)

    partial = jnp.dot(hidden_z, down_weight, preferred_element_type=F32).astype(BF)
    out_z = lax.psum_scatter(partial, ("zh", "zl"), scatter_dimension=0, tiled=True)
    _, other_z, hidden_near, hidden_far = tie((partial, other_z, hidden_near, hidden_far))
    even = lax.axis_index("zl") == 0
    ours, theirs = [rows_z.reshape(NZH, NC * both, -1) for rows_z in (mine_z, other_z)]
    near = jnp.stack([jnp.where(even, ours, theirs), jnp.where(even, theirs, ours)], axis=1)
    near = near.reshape(NC * tok, -1)
    hidden_all = jnp.concatenate([hidden_near.reshape(NC * tok, ff), hidden_far], axis=1)

    grad_acc = lax.dot_general(
        near, hidden_all, (((0,), (0,)), ((), ())), preferred_element_type=F32
    )
    term = (grad_acc / (NX * NYH * NC)).astype(BF).reshape(NX, NYH * half, NYL * ff)
    term, near, gate_pre, up_pre, weight = tie((term, near, gate_pre, up_pre, down_weight))
    by_x = lax.all_to_all(term, "x", 0, 0)

    far = lax.ppermute(near, "yl", SWAP)
    weight_near, weight_far = weight_quarters(place, weight)
    back = lax.dot_general(near, weight_near, across, preferred_element_type=F32)
    sum_x = by_x.astype(F32).sum(0).astype(BF).reshape(NYH, half, NYL, ff)
    own, other = sum_x[:, :, 0], sum_x[:, :, 1]
    sum_x = jnp.stack([jnp.where(first, own, other), jnp.where(first, other, own)], axis=1)
    sum_x, far, back = tie((sum_x, far, back))
    back = back + lax.dot_general(far, weight_far, across, preferred_element_type=F32)
    back = back.reshape(NZ, NC, both, ff)
    back_z = back[:, 0] + lax.ppermute(back[:, 1], "c", SWAP)
    back = back_z.reshape(NZ, NYL, rows, ff).transpose(1, 0, 2, 3).reshape(tok, ff)
    gate_wide = gate_pre.astype(F32)
    up_wide = up_pre.astype(F32)
    sig = jax.nn.sigmoid(gate_wide)
    act = gate_wide * sig
    gate_grad = (back * up_wide * sig * (1.0 + gate_wide * (1.0 - sig))).astype(BF)
    up_grad = (back * act).astype(BF)

    by_y = lax.all_to_all(sum_x.reshape(NYH * NYL, half, ff), ("yh", "yl"), 0, 0)
    by_y = by_y.reshape(NYH, NYL * half, ff)
    weight_grad = by_y.astype(F32).sum(0).astype(BF).T

    keep = lax.dynamic_slice_in_dim(out_z, yl * rows, rows, 0)
    give = lax.dynamic_slice_in_dim(out_z, (1 - yl) * rows, rows, 0)
    got = lax.ppermute(give, "yl", SWAP)
    output = (keep.astype(F32) + got.astype(F32)).astype(BF)
    return output, gate_grad, up_grad, weight_grad


def solution(mesh):
    fine = Mesh(
        mesh.devices.reshape(NX, NYH, NC, NYL, NZH, NZL), ("x", "yh", "c", "yl", "zh", "zl")
    )
    dp, tensor = ("x", "yh", "c"), ("yl", "zh", "zl")
    return jax.shard_map(
        per_device,
        mesh=fine,
        in_specs=(P(dp, tensor), P(dp, tensor), P(tensor, None), P(dp + tensor, None)),
        out_specs=(P(dp + tensor, None), P(dp, tensor), P(dp, tensor), P(tensor, dp)),
        check_vma=False,
    )
```

```python
import jax
import jax.numpy as jnp
from jax import lax
from jax.experimental import pallas as pl
from jax.experimental.pallas import tpu as pltpu
from jax.sharding import Mesh, PartitionSpec as P

NX, NYH, NC, NYL, NZH, NZL = 4, 4, 2, 2, 6, 2
NZ = NZH * NZL
NB = NX * NYH
BF, F32 = jnp.bfloat16, jnp.float32
SWAP = [(0, 1), (1, 0)]
DIAGONAL = [(0, 3), (1, 2), (2, 1), (3, 0)]
tie = lax.optimization_barrier


def quarter(ref, core, yl):
    lane = ref.shape[1] // (NB * NC)
    half = lane // NYL
    pieces = []
    for pair in range(NB):
        at = (pair * NC + core) * lane
        pieces.append(ref[:, at : at + lane][:, yl * half : (yl + 1) * half])
    return jnp.concatenate(pieces, axis=1)


def split_kernel(place_ref, cot_ref, *out_refs):
    for core in range(NC):
        for yl in range(NYL):

            @pl.when(place_ref[0] == core * NYL + yl)
            def _():
                wanted = ((core, yl), (1 - core, yl), (core, 1 - yl), (1 - core, 1 - yl))
                for out_ref, (c, y) in zip(out_refs, wanted):
                    out_ref[...] = quarter(cot_ref, c, y)


def split_columns(place, cot):
    rows, feat = cot.shape
    vmem = pl.BlockSpec(memory_space=pltpu.VMEM)
    return pl.pallas_call(
        split_kernel,
        out_shape=[jax.ShapeDtypeStruct((rows, feat // 4), cot.dtype)] * 4,
        in_specs=[pl.BlockSpec(memory_space=pltpu.SMEM), vmem],
        out_specs=[vmem] * 4,
        name="split_columns",
    )(place, cot)


def weight_kernel(place_ref, weight_ref, near_ref, far_ref):
    for core in range(NC):
        for yl in range(NYL):

            @pl.when(place_ref[0] == core * NYL + yl)
            def _():
                near_ref[...] = quarter(weight_ref, core, yl)
                far_ref[...] = quarter(weight_ref, core, 1 - yl)


def weight_quarters(place, weight):
    ff, feat = weight.shape
    step = 128
    return pl.pallas_call(
        weight_kernel,
        out_shape=[jax.ShapeDtypeStruct((ff, feat // 4), weight.dtype)] * 2,
        grid=(ff // step,),
        in_specs=[
            pl.BlockSpec(memory_space=pltpu.SMEM),
            pl.BlockSpec((step, feat), lambda i: (i, 0)),
        ],
        out_specs=[pl.BlockSpec((step, feat // 4), lambda i: (i, 0))] * 2,
        name="weight_quarters",
    )(place, weight)


def per_device(gate_pre, up_pre, down_weight, cotangent):
    tok, ff = gate_pre.shape
    rows, feat = cotangent.shape
    block = feat // (NB * NC)
    half = block // NYL
    both = NYL * rows
    core, yl = lax.axis_index("c"), lax.axis_index("yl")
    first = yl == 0
    place = (core * NYL + yl).reshape(1)
    across = (((1,), (1,)), ((), ()))

    mine, to_core, to_yl, to_diag = split_columns(place, cotangent)
    from_core = lax.ppermute(to_core, "c", SWAP)
    from_yl = lax.ppermute(to_yl, "yl", SWAP)
    from_diag = lax.ppermute(to_diag, ("c", "yl"), DIAGONAL)

    gate_wide = gate_pre.astype(F32)
    up_wide = up_pre.astype(F32)
    sig = jax.nn.sigmoid(gate_wide)
    act = gate_wide * sig
    hidden = (act * up_wide).astype(BF)
    hidden_z = hidden.reshape(NYL, NZ, rows, ff).transpose(1, 0, 2, 3).reshape(tok, ff)
    hidden_z, from_core, from_yl, from_diag = tie((hidden_z, from_core, from_yl, from_diag))
    hidden_core = lax.ppermute(hidden_z, "c", SWAP)

    shard = jnp.concatenate(
        [
            jnp.where(first, mine, from_yl),
            jnp.where(first, from_yl, mine),
            jnp.where(first, from_core, from_diag),
            jnp.where(first, from_diag, from_core),
        ],
        axis=0,
    )
    hidden_near = jnp.stack([h.reshape(NZ, both, ff) for h in (hidden_z, hidden_core)], axis=1)
    shard, hidden_near, hidden_z = tie((shard, hidden_near, hidden_z))
    hidden_far = lax.ppermute(hidden_near.reshape(NC * tok, ff), "yl", SWAP)
    mine_z = lax.all_gather(shard, "zh", axis=0, tiled=True)
    mine_z, hidden_z, hidden_far = tie((mine_z, hidden_z, hidden_far))
    other_z = lax.ppermute(mine_z, "zl", SWAP)
    mine_far = lax.ppermute(mine_z, "yl", SWAP)

    partial = jnp.dot(hidden_z, down_weight, preferred_element_type=F32).astype(BF)
    out_z = lax.psum_scatter(partial, ("zh", "zl"), scatter_dimension=0, tiled=True)
    _, mine_far, other_z, hidden_near, hidden_far = tie(
        (partial, mine_far, other_z, hidden_near, hidden_far)
    )
    even = lax.axis_index("zl") == 0

    def by_place(ours, theirs):
        ours, theirs = [rows_z.reshape(NZH, NC * both, -1) for rows_z in (ours, theirs)]
        pair = [jnp.where(even, ours, theirs), jnp.where(even, theirs, ours)]
        return jnp.stack(pair, axis=1).reshape(NC * tok, -1)

    near = by_place(mine_z, other_z)
    hidden_all = jnp.concatenate([hidden_near.reshape(NC * tok, ff), hidden_far], axis=1)

    grad_acc = lax.dot_general(
        near, hidden_all, (((0,), (0,)), ((), ())), preferred_element_type=F32
    )
    term = (grad_acc / (NX * NYH * NC)).astype(BF).reshape(NX, NYH * half, NYL * ff)
    term, near, other_z, mine_far, gate_pre, up_pre, weight = tie(
        (term, near, other_z, mine_far, gate_pre, up_pre, down_weight)
    )
    by_x = lax.all_to_all(term, "x", 0, 0)

    far = by_place(mine_far, lax.ppermute(other_z, "yl", SWAP))
    weight_near, weight_far = weight_quarters(place, weight)
    back = lax.dot_general(near, weight_near, across, preferred_element_type=F32)
    back = back + lax.dot_general(far, weight_far, across, preferred_element_type=F32)
    back = back.reshape(NZ, NC, both, ff)
    by_x, back = tie((by_x, back))
    sum_x = by_x.astype(F32).sum(0).astype(BF).reshape(NYH, half, NYL, ff)
    own, other = sum_x[:, :, 0], sum_x[:, :, 1]
    sum_x = jnp.stack([jnp.where(first, own, other), jnp.where(first, other, own)], axis=1)
    back_z = back[:, 0] + lax.ppermute(back[:, 1], "c", SWAP)
    back = back_z.reshape(NZ, NYL, rows, ff).transpose(1, 0, 2, 3).reshape(tok, ff)
    gate_wide = gate_pre.astype(F32)
    up_wide = up_pre.astype(F32)
    sig = jax.nn.sigmoid(gate_wide)
    act = gate_wide * sig
    gate_grad = (back * up_wide * sig * (1.0 + gate_wide * (1.0 - sig))).astype(BF)
    up_grad = (back * act).astype(BF)

    by_y = lax.all_to_all(sum_x.reshape(NYH * NYL, half, ff), ("yh", "yl"), 0, 0)
    by_y = by_y.reshape(NYH, NYL * half, ff)
    weight_grad = by_y.astype(F32).sum(0).astype(BF).T

    keep = lax.dynamic_slice_in_dim(out_z, yl * rows, rows, 0)
    give = lax.dynamic_slice_in_dim(out_z, (1 - yl) * rows, rows, 0)
    got = lax.ppermute(give, "yl", SWAP)
    output = (keep.astype(F32) + got.astype(F32)).astype(BF)
    return output, gate_grad, up_grad, weight_grad


def solution(mesh):
    fine = Mesh(
        mesh.devices.reshape(NX, NYH, NC, NYL, NZH, NZL), ("x", "yh", "c", "yl", "zh", "zl")
    )
    dp, tensor = ("x", "yh", "c"), ("yl", "zh", "zl")
    return jax.shard_map(
        per_device,
        mesh=fine,
        in_specs=(P(dp, tensor), P(dp, tensor), P(tensor, None), P(dp + tensor, None)),
        out_specs=(P(dp + tensor, None), P(dp, tensor), P(dp, tensor), P(tensor, dp)),
        check_vma=False,
    )
```

```python
import jax
import jax.numpy as jnp
from jax import lax
from jax.experimental import pallas as pl
from jax.experimental.pallas import tpu as pltpu
from jax.sharding import Mesh, PartitionSpec as P

NX, NYH, NC, NYL, NZH, NZL = 4, 4, 2, 2, 6, 2
NZ = NZH * NZL
NB = NX * NYH
BF, F32 = jnp.bfloat16, jnp.float32
SWAP = [(0, 1), (1, 0)]
DIAGONAL = [(0, 3), (1, 2), (2, 1), (3, 0)]
tie = lax.optimization_barrier


def quarter(ref, core, yl):
    lane = ref.shape[1] // (NB * NC)
    half = lane // NYL
    pieces = []
    for pair in range(NB):
        at = (pair * NC + core) * lane
        pieces.append(ref[:, at : at + lane][:, yl * half : (yl + 1) * half])
    return jnp.concatenate(pieces, axis=1)


def split_kernel(place_ref, cot_ref, *out_refs):
    for core in range(NC):
        for yl in range(NYL):

            @pl.when(place_ref[0] == core * NYL + yl)
            def _():
                wanted = ((core, yl), (1 - core, yl), (core, 1 - yl), (1 - core, 1 - yl))
                for out_ref, (c, y) in zip(out_refs, wanted):
                    out_ref[...] = quarter(cot_ref, c, y)


def split_columns(place, cot):
    rows, feat = cot.shape
    vmem = pl.BlockSpec(memory_space=pltpu.VMEM)
    return pl.pallas_call(
        split_kernel,
        out_shape=[jax.ShapeDtypeStruct((rows, feat // 4), cot.dtype)] * 4,
        in_specs=[pl.BlockSpec(memory_space=pltpu.SMEM), vmem],
        out_specs=[vmem] * 4,
        name="split_columns",
    )(place, cot)


def weight_kernel(place_ref, weight_ref, near_ref, far_ref):
    for core in range(NC):
        for yl in range(NYL):

            @pl.when(place_ref[0] == core * NYL + yl)
            def _():
                near_ref[...] = quarter(weight_ref, core, yl)
                far_ref[...] = quarter(weight_ref, core, 1 - yl)


def weight_quarters(place, weight):
    ff, feat = weight.shape
    step = 128
    return pl.pallas_call(
        weight_kernel,
        out_shape=[jax.ShapeDtypeStruct((ff, feat // 4), weight.dtype)] * 2,
        grid=(ff // step,),
        in_specs=[
            pl.BlockSpec(memory_space=pltpu.SMEM),
            pl.BlockSpec((step, feat), lambda i: (i, 0)),
        ],
        out_specs=[pl.BlockSpec((step, feat // 4), lambda i: (i, 0))] * 2,
        name="weight_quarters",
    )(place, weight)


def per_device(gate_pre, up_pre, down_weight, cotangent):
    tok, ff = gate_pre.shape
    rows, feat = cotangent.shape
    block = feat // (NB * NC)
    half = block // NYL
    both = NYL * rows
    core, yl = lax.axis_index("c"), lax.axis_index("yl")
    first = yl == 0
    place = (core * NYL + yl).reshape(1)
    across = (((1,), (1,)), ((), ()))

    mine, to_core, to_yl, to_diag = split_columns(place, cotangent)
    from_core = lax.ppermute(to_core, "c", SWAP)
    from_yl = lax.ppermute(to_yl, "yl", SWAP)
    from_diag = lax.ppermute(to_diag, ("c", "yl"), DIAGONAL)

    gate_wide = gate_pre.astype(F32)
    up_wide = up_pre.astype(F32)
    sig = jax.nn.sigmoid(gate_wide)
    act = gate_wide * sig
    hidden = (act * up_wide).astype(BF)
    hidden_z = hidden.reshape(NYL, NZ, rows, ff).transpose(1, 0, 2, 3).reshape(tok, ff)
    hidden_z, from_core, from_yl, from_diag = tie((hidden_z, from_core, from_yl, from_diag))
    hidden_core = lax.ppermute(hidden_z, "c", SWAP)

    shard = jnp.concatenate(
        [
            jnp.where(first, mine, from_yl),
            jnp.where(first, from_yl, mine),
            jnp.where(first, from_core, from_diag),
            jnp.where(first, from_diag, from_core),
        ],
        axis=0,
    )
    hidden_near = jnp.stack([h.reshape(NZ, both, ff) for h in (hidden_z, hidden_core)], axis=1)
    shard, hidden_near, hidden_z = tie((shard, hidden_near, hidden_z))
    hidden_far = lax.ppermute(hidden_near.reshape(NC * tok, ff), "yl", SWAP)
    mine_z = lax.all_gather(shard, "zh", axis=0, tiled=True)
    mine_z, hidden_z, hidden_far = tie((mine_z, hidden_z, hidden_far))
    other_z = lax.ppermute(mine_z, "zl", SWAP)

    partial = jnp.dot(hidden_z, down_weight, preferred_element_type=F32).astype(BF)
    out_z = lax.psum_scatter(partial, ("zh", "zl"), scatter_dimension=0, tiled=True)
    hidden_near = hidden_near.reshape(NC * tok, ff)
    hidden_all = jnp.concatenate(
        [jnp.where(first, hidden_near, hidden_far), jnp.where(first, hidden_far, hidden_near)],
        axis=1,
    )
    _, other_z, hidden_all = tie((partial, other_z, hidden_all))
    even = lax.axis_index("zl") == 0
    ours, theirs = [rows_z.reshape(NZH, NC * both, -1) for rows_z in (mine_z, other_z)]
    near = jnp.stack([jnp.where(even, ours, theirs), jnp.where(even, theirs, ours)], axis=1)
    near = near.reshape(NC * tok, -1)

    grad_acc = lax.dot_general(
        near, hidden_all, (((0,), (0,)), ((), ())), preferred_element_type=F32
    )
    term = (grad_acc / (NX * NYH * NC)).astype(BF).reshape(NX, NYH * half, NYL * ff)
    term, near, gate_pre, up_pre, weight = tie((term, near, gate_pre, up_pre, down_weight))
    by_x = lax.all_to_all(term, "x", 0, 0)

    far = lax.ppermute(near, "yl", SWAP)
    weight_near, weight_far = weight_quarters(place, weight)
    back = lax.dot_general(near, weight_near, across, preferred_element_type=F32)
    sum_x = by_x.astype(F32).sum(0).astype(BF).reshape(NYH, half, NYL, ff)
    sum_x = sum_x.transpose(0, 2, 1, 3).reshape(NYH * NYL, half, ff)
    sum_x, far, back = tie((sum_x, far, back))
    back = back + lax.dot_general(far, weight_far, across, preferred_element_type=F32)
    back = back.reshape(NZ, NC, both, ff)
    back_z = back[:, 0] + lax.ppermute(back[:, 1], "c", SWAP)
    back = back_z.reshape(NZ, NYL, rows, ff).transpose(1, 0, 2, 3).reshape(tok, ff)
    gate_wide = gate_pre.astype(F32)
    up_wide = up_pre.astype(F32)
    sig = jax.nn.sigmoid(gate_wide)
    act = gate_wide * sig
    gate_grad = (back * up_wide * sig * (1.0 + gate_wide * (1.0 - sig))).astype(BF)
    up_grad = (back * act).astype(BF)

    by_y = lax.all_to_all(sum_x, ("yh", "yl"), 0, 0)
    by_y = by_y.reshape(NYH, NYL * half, ff)
    weight_grad = by_y.astype(F32).sum(0).astype(BF).T

    keep = lax.dynamic_slice_in_dim(out_z, yl * rows, rows, 0)
    give = lax.dynamic_slice_in_dim(out_z, (1 - yl) * rows, rows, 0)
    got = lax.ppermute(give, "yl", SWAP)
    output = (keep.astype(F32) + got.astype(F32)).astype(BF)
    return output, gate_grad, up_grad, weight_grad


def solution(mesh):
    fine = Mesh(
        mesh.devices.reshape(NX, NYH, NC, NYL, NZH, NZL), ("x", "yh", "c", "yl", "zh", "zl")
    )
    dp, tensor = ("x", "yh", "c"), ("yl", "zh", "zl")
    return jax.shard_map(
        per_device,
        mesh=fine,
        in_specs=(P(dp, tensor), P(dp, tensor), P(tensor, None), P(dp + tensor, None)),
        out_specs=(P(dp + tensor, None), P(dp, tensor), P(dp, tensor), P(tensor, dp)),
        check_vma=False,
    )
```

```python
import jax
import jax.numpy as jnp
from jax import lax
from jax.experimental import pallas as pl
from jax.experimental.pallas import tpu as pltpu
from jax.sharding import Mesh, PartitionSpec as P

NX, NYH, NC, NYL, NZH, NZL = 4, 4, 2, 2, 6, 2
NZ = NZH * NZL
NB = NX * NYH
BF, F32 = jnp.bfloat16, jnp.float32
SWAP = [(0, 1), (1, 0)]
tie = lax.optimization_barrier


def quarter(ref, core, yl):
    lane = ref.shape[1] // (NB * NC)
    half = lane // NYL
    pieces = []
    for pair in range(NB):
        at = (pair * NC + core) * lane
        pieces.append(ref[:, at : at + lane][:, yl * half : (yl + 1) * half])
    return jnp.concatenate(pieces, axis=1)


def split_kernel(place_ref, cot_ref, *out_refs):
    for core in range(NC):
        for yl in range(NYL):

            @pl.when(place_ref[0] == core * NYL + yl)
            def _():
                wanted = ((core, yl), (1 - core, yl), (core, 1 - yl), (1 - core, 1 - yl))
                for out_ref, (c, y) in zip(out_refs, wanted):
                    out_ref[...] = quarter(cot_ref, c, y)


def split_columns(place, cot):
    rows, feat = cot.shape
    vmem = pl.BlockSpec(memory_space=pltpu.VMEM)
    return pl.pallas_call(
        split_kernel,
        out_shape=[jax.ShapeDtypeStruct((rows, feat // 4), cot.dtype)] * 4,
        in_specs=[pl.BlockSpec(memory_space=pltpu.SMEM), vmem],
        out_specs=[vmem] * 4,
        name="split_columns",
    )(place, cot)


def weight_kernel(place_ref, weight_ref, near_ref, far_ref):
    for core in range(NC):
        for yl in range(NYL):

            @pl.when(place_ref[0] == core * NYL + yl)
            def _():
                near_ref[...] = quarter(weight_ref, core, yl)
                far_ref[...] = quarter(weight_ref, core, 1 - yl)


def weight_quarters(place, weight):
    ff, feat = weight.shape
    step = 128
    return pl.pallas_call(
        weight_kernel,
        out_shape=[jax.ShapeDtypeStruct((ff, feat // 4), weight.dtype)] * 2,
        grid=(ff // step,),
        in_specs=[
            pl.BlockSpec(memory_space=pltpu.SMEM),
            pl.BlockSpec((step, feat), lambda i: (i, 0)),
        ],
        out_specs=[pl.BlockSpec((step, feat // 4), lambda i: (i, 0))] * 2,
        name="weight_quarters",
    )(place, weight)


def per_device(gate_pre, up_pre, down_weight, cotangent):
    tok, ff = gate_pre.shape
    rows, feat = cotangent.shape
    block = feat // (NB * NC)
    half = block // NYL
    both = NYL * rows
    core, yl = lax.axis_index("c"), lax.axis_index("yl")
    first = yl == 0
    place = (core * NYL + yl).reshape(1)
    across = (((1,), (1,)), ((), ()))

    mine, to_core, to_yl, to_diag = split_columns(place, cotangent)
    from_core = lax.ppermute(jnp.concatenate([to_core, to_diag], axis=0), "c", SWAP)

    gate_wide = gate_pre.astype(F32)
    up_wide = up_pre.astype(F32)
    sig = jax.nn.sigmoid(gate_wide)
    act = gate_wide * sig
    hidden = (act * up_wide).astype(BF)
    hidden_z = hidden.reshape(NYL, NZ, rows, ff).transpose(1, 0, 2, 3).reshape(tok, ff)
    hidden_core = lax.ppermute(hidden_z, "c", SWAP)
    hidden_z, from_core = tie((hidden_z, from_core))
    mine_both = jnp.concatenate([mine, from_core[:rows]], axis=0)
    from_yl = lax.ppermute(jnp.concatenate([to_yl, from_core[rows:]], axis=0), "yl", SWAP)

    low, high = jnp.where(first, mine_both, from_yl), jnp.where(first, from_yl, mine_both)
    shard = jnp.concatenate([low[:rows], high[:rows], low[rows:], high[rows:]], axis=0)
    hidden_near = jnp.stack([h.reshape(NZ, both, ff) for h in (hidden_z, hidden_core)], axis=1)
    shard, hidden_near, hidden_z = tie((shard, hidden_near, hidden_z))
    hidden_far = lax.ppermute(hidden_near.reshape(NC * tok, ff), "yl", SWAP)
    mine_z = lax.all_gather(shard, "zh", axis=0, tiled=True)
    mine_z, hidden_z, hidden_far = tie((mine_z, hidden_z, hidden_far))
    other_z = lax.ppermute(mine_z, "zl", SWAP)

    partial = jnp.dot(hidden_z, down_weight, preferred_element_type=F32).astype(BF)
    out_z = lax.psum_scatter(partial, ("zh", "zl"), scatter_dimension=0, tiled=True)
    hidden_near = hidden_near.reshape(NC * tok, ff)
    hidden_all = jnp.concatenate(
        [jnp.where(first, hidden_near, hidden_far), jnp.where(first, hidden_far, hidden_near)],
        axis=1,
    )
    _, other_z, hidden_all = tie((partial, other_z, hidden_all))
    even = lax.axis_index("zl") == 0
    ours, theirs = [rows_z.reshape(NZH, NC * both, -1) for rows_z in (mine_z, other_z)]
    near = jnp.stack([jnp.where(even, ours, theirs), jnp.where(even, theirs, ours)], axis=1)
    near = near.reshape(NC * tok, -1)

    grad_acc = lax.dot_general(
        near, hidden_all, (((0,), (0,)), ((), ())), preferred_element_type=F32
    )
    term = (grad_acc / (NX * NYH * NC)).astype(BF).reshape(NX, NYH * half, NYL * ff)
    term, near, gate_pre, up_pre, weight = tie((term, near, gate_pre, up_pre, down_weight))
    by_x = lax.all_to_all(term, "x", 0, 0)

    far = lax.ppermute(near, "yl", SWAP)
    weight_near, weight_far = weight_quarters(place, weight)
    back = lax.dot_general(near, weight_near, across, preferred_element_type=F32)
    sum_x = by_x.astype(F32).sum(0).astype(BF).reshape(NYH, half, NYL, ff)
    sum_x = sum_x.transpose(0, 2, 1, 3).reshape(NYH * NYL, half, ff)
    sum_x, far, back = tie((sum_x, far, back))
    back = back + lax.dot_general(far, weight_far, across, preferred_element_type=F32)
    back = back.reshape(NZ, NC, both, ff)
    back_z = back[:, 0] + lax.ppermute(back[:, 1], "c", SWAP)
    back = back_z.reshape(NZ, NYL, rows, ff).transpose(1, 0, 2, 3).reshape(tok, ff)
    gate_wide = gate_pre.astype(F32)
    up_wide = up_pre.astype(F32)
    sig = jax.nn.sigmoid(gate_wide)
    act = gate_wide * sig
    gate_grad = (back * up_wide * sig * (1.0 + gate_wide * (1.0 - sig))).astype(BF)
    up_grad = (back * act).astype(BF)

    by_y = lax.all_to_all(sum_x, ("yh", "yl"), 0, 0)
    by_y = by_y.reshape(NYH, NYL * half, ff)
    weight_grad = by_y.astype(F32).sum(0).astype(BF).T

    keep = lax.dynamic_slice_in_dim(out_z, yl * rows, rows, 0)
    give = lax.dynamic_slice_in_dim(out_z, (1 - yl) * rows, rows, 0)
    got = lax.ppermute(give, "yl", SWAP)
    output = (keep.astype(F32) + got.astype(F32)).astype(BF)
    return output, gate_grad, up_grad, weight_grad


def solution(mesh):
    fine = Mesh(
        mesh.devices.reshape(NX, NYH, NC, NYL, NZH, NZL), ("x", "yh", "c", "yl", "zh", "zl")
    )
    dp, tensor = ("x", "yh", "c"), ("yl", "zh", "zl")
    return jax.shard_map(
        per_device,
        mesh=fine,
        in_specs=(P(dp, tensor), P(dp, tensor), P(tensor, None), P(dp + tensor, None)),
        out_specs=(P(dp + tensor, None), P(dp, tensor), P(dp, tensor), P(tensor, dp)),
        check_vma=False,
    )
```

```python
import jax
import jax.numpy as jnp
from jax import lax
from jax.experimental import pallas as pl
from jax.experimental.pallas import tpu as pltpu
from jax.sharding import Mesh, PartitionSpec as P

NX, NYH, NC, NYL, NZH, NZL = 4, 4, 2, 2, 6, 2
NZ = NZH * NZL
NB = NX * NYH
BF, F32 = jnp.bfloat16, jnp.float32
SWAP = [(0, 1), (1, 0)]
tie = lax.optimization_barrier


def quarter(ref, core, yl):
    lane = ref.shape[1] // (NB * NC)
    half = lane // NYL
    pieces = []
    for pair in range(NB):
        at = (pair * NC + core) * lane
        pieces.append(ref[:, at : at + lane][:, yl * half : (yl + 1) * half])
    return jnp.concatenate(pieces, axis=1)


def split_kernel(place_ref, cot_ref, *out_refs):
    for core in range(NC):
        for yl in range(NYL):

            @pl.when(place_ref[0] == core * NYL + yl)
            def _():
                mine_ref, yl_ref, core_ref = out_refs
                width = mine_ref.shape[1]
                mine_ref[...] = quarter(cot_ref, core, yl)
                yl_ref[...] = quarter(cot_ref, core, 1 - yl)
                core_ref[:, :width] = quarter(cot_ref, 1 - core, yl)
                core_ref[:, width:] = quarter(cot_ref, 1 - core, 1 - yl)


def split_columns(place, cot):
    rows, feat = cot.shape
    vmem = pl.BlockSpec(memory_space=pltpu.VMEM)
    return pl.pallas_call(
        split_kernel,
        out_shape=[jax.ShapeDtypeStruct((rows, feat // n), cot.dtype) for n in (4, 4, 2)],
        in_specs=[pl.BlockSpec(memory_space=pltpu.SMEM), vmem],
        out_specs=[vmem] * 3,
        name="split_columns",
    )(place, cot)


def weight_kernel(place_ref, weight_ref, near_ref, far_ref):
    for core in range(NC):
        for yl in range(NYL):

            @pl.when(place_ref[0] == core * NYL + yl)
            def _():
                near_ref[...] = quarter(weight_ref, core, yl)
                far_ref[...] = quarter(weight_ref, core, 1 - yl)


def weight_quarters(place, weight):
    ff, feat = weight.shape
    step = 128
    return pl.pallas_call(
        weight_kernel,
        out_shape=[jax.ShapeDtypeStruct((ff, feat // 4), weight.dtype)] * 2,
        grid=(ff // step,),
        in_specs=[
            pl.BlockSpec(memory_space=pltpu.SMEM),
            pl.BlockSpec((step, feat), lambda i: (i, 0)),
        ],
        out_specs=[pl.BlockSpec((step, feat // 4), lambda i: (i, 0))] * 2,
        name="weight_quarters",
    )(place, weight)


def per_device(gate_pre, up_pre, down_weight, cotangent):
    tok, ff = gate_pre.shape
    rows, feat = cotangent.shape
    block = feat // (NB * NC)
    half = block // NYL
    both = NYL * rows
    core, yl = lax.axis_index("c"), lax.axis_index("yl")
    first = yl == 0
    place = (core * NYL + yl).reshape(1)
    across = (((1,), (1,)), ((), ()))

    mine, to_yl, to_core = split_columns(place, cotangent)
    from_core = lax.ppermute(to_core, "c", SWAP)
    width = mine.shape[1]

    gate_wide = gate_pre.astype(F32)
    up_wide = up_pre.astype(F32)
    sig = jax.nn.sigmoid(gate_wide)
    act = gate_wide * sig
    hidden = (act * up_wide).astype(BF)
    hidden_z = hidden.reshape(NYL, NZ, rows, ff).transpose(1, 0, 2, 3).reshape(tok, ff)
    hidden_core = lax.ppermute(hidden_z, "c", SWAP)
    hidden_z, from_core = tie((hidden_z, from_core))
    mine_both = jnp.concatenate([mine, from_core[:, :width]], axis=0)
    from_yl = lax.ppermute(jnp.concatenate([to_yl, from_core[:, width:]], axis=0), "yl", SWAP)

    low, high = jnp.where(first, mine_both, from_yl), jnp.where(first, from_yl, mine_both)
    shard = jnp.concatenate([low[:rows], high[:rows], low[rows:], high[rows:]], axis=0)
    hidden_near = jnp.stack([h.reshape(NZ, both, ff) for h in (hidden_z, hidden_core)], axis=1)
    shard, hidden_near, hidden_z = tie((shard, hidden_near, hidden_z))
    hidden_far = lax.ppermute(hidden_near.reshape(NC * tok, ff), "yl", SWAP)
    mine_z = lax.all_gather(shard, "zh", axis=0, tiled=True)
    mine_z, hidden_z, hidden_far = tie((mine_z, hidden_z, hidden_far))
    other_z = lax.ppermute(mine_z, "zl", SWAP)

    partial = jnp.dot(hidden_z, down_weight, preferred_element_type=F32).astype(BF)
    out_z = lax.psum_scatter(partial, ("zh", "zl"), scatter_dimension=0, tiled=True)
    hidden_near = hidden_near.reshape(NC * tok, ff)
    hidden_all = jnp.concatenate(
        [jnp.where(first, hidden_near, hidden_far), jnp.where(first, hidden_far, hidden_near)],
        axis=1,
    )
    _, other_z, hidden_all = tie((partial, other_z, hidden_all))
    even = lax.axis_index("zl") == 0
    ours, theirs = [rows_z.reshape(NZH, NC * both, -1) for rows_z in (mine_z, other_z)]
    near = jnp.stack([jnp.where(even, ours, theirs), jnp.where(even, theirs, ours)], axis=1)
    near = near.reshape(NC * tok, -1)

    grad_acc = lax.dot_general(
        near, hidden_all, (((0,), (0,)), ((), ())), preferred_element_type=F32
    )
    term = (grad_acc / (NX * NYH * NC)).astype(BF).reshape(NX, NYH * half, NYL * ff)
    term, near, gate_pre, up_pre, weight = tie((term, near, gate_pre, up_pre, down_weight))
    by_x = lax.all_to_all(term, "x", 0, 0)

    far = lax.ppermute(near, "yl", SWAP)
    weight_near, weight_far = weight_quarters(place, weight)
    back = lax.dot_general(near, weight_near, across, preferred_element_type=F32)
    sum_x = by_x.astype(F32).sum(0).astype(BF).reshape(NYH, half, NYL, ff)
    sum_x = sum_x.transpose(0, 2, 1, 3).reshape(NYH * NYL, half, ff)
    sum_x, far, back = tie((sum_x, far, back))
    back = back + lax.dot_general(far, weight_far, across, preferred_element_type=F32)
    back = back.reshape(NZ, NC, both, ff)
    back_z = back[:, 0] + lax.ppermute(back[:, 1], "c", SWAP)
    back = back_z.reshape(NZ, NYL, rows, ff).transpose(1, 0, 2, 3).reshape(tok, ff)
    gate_wide = gate_pre.astype(F32)
    up_wide = up_pre.astype(F32)
    sig = jax.nn.sigmoid(gate_wide)
    act = gate_wide * sig
    gate_grad = (back * up_wide * sig * (1.0 + gate_wide * (1.0 - sig))).astype(BF)
    up_grad = (back * act).astype(BF)

    by_y = lax.all_to_all(sum_x, ("yh", "yl"), 0, 0)
    by_y = by_y.reshape(NYH, NYL * half, ff)
    weight_grad = by_y.astype(F32).sum(0).astype(BF).T

    keep = lax.dynamic_slice_in_dim(out_z, yl * rows, rows, 0)
    give = lax.dynamic_slice_in_dim(out_z, (1 - yl) * rows, rows, 0)
    got = lax.ppermute(give, "yl", SWAP)
    output = (keep.astype(F32) + got.astype(F32)).astype(BF)
    return output, gate_grad, up_grad, weight_grad


def solution(mesh):
    fine = Mesh(
        mesh.devices.reshape(NX, NYH, NC, NYL, NZH, NZL), ("x", "yh", "c", "yl", "zh", "zl")
    )
    dp, tensor = ("x", "yh", "c"), ("yl", "zh", "zl")
    return jax.shard_map(
        per_device,
        mesh=fine,
        in_specs=(P(dp, tensor), P(dp, tensor), P(tensor, None), P(dp + tensor, None)),
        out_specs=(P(dp + tensor, None), P(dp, tensor), P(dp, tensor), P(tensor, dp)),
        check_vma=False,
    )
```
